256 devices in a mesh: stretch: 64 (over x, z_lo, y), head: 4 (over z_hi, core).
Axes of the slice: x: 4, y: 4, z: 8 (z_hi: 2, z_lo: 4; z = z_hi * 4 + z_lo), core: 2. Of those that a mesh axis runs over, the one named last changes fastest.
Arguments:
- queries: bfloat16 [8192, 6144], P('stretch', 'head'), may hold values from -92 to 92
- keys: bfloat16 [8192, 1024], P('stretch', 'head'), may hold values from -11 to 11
- values: bfloat16 [8192, 1024], P('stretch', 'head'), may hold values from -6 to 6
- cache_keys: bfloat16 [4096, 1024], P(('stretch', 'head')), may hold values from -100 to 100
- cache_values: bfloat16 [4096, 1024], P(('stretch', 'head')), may hold values from -6 to 6
- page_owner: int32 [64], replicated, may hold values from 0 to 63, each once
- window: int32 [4], replicated, may hold values from 1 to 2, as said below
Outputs:
- attended: bfloat16 [8192, 6144], P('stretch', 'head')
The draws below stay inside these ranges and needn't reach their ends.
Inputs may be any that keep to these rules, and one draw needn't show every extreme that they name: `window`: some in-flight stretch attends all 2 cached stretches.
All inputs are finite; a program needn't handle non-finite values.
Results may differ from the reference program's by a relative error of at most 0.006.
Values may be sent and summed in bfloat16 or wider, within the bound.
No kernel may reach another device: no remote copies, remote signals or barrier semaphores. Data moves between devices by JAX's collectives and lax.ppermute only.
A program may use at most 192 MiB of HBM per device.

```python
import jax
import jax.numpy as jnp
from jax import lax

HEADS = 48
KV_HEADS = 8
D_HEAD = 128
TOK_DEV = 128
STRETCHES = 4
CACHED = 2
CACHE_DEV = 64
PAGES = 64
TOKENS = 8192
CACHE_TOK = 4096


def shared_keys(key):
    return 1.6 * jax.random.truncated_normal(key, -6.0, 6.0, (TOKENS, KV_HEADS * D_HEAD), jnp.float32)


def shared_pattern(key):
    key = jax.random.fold_in(key, 201)
    sign_key, size_key, channel_key, offset_key, other_key = jax.random.split(key, 5)
    signs = jnp.where(jax.random.bernoulli(sign_key, 0.5, (KV_HEADS, D_HEAD)), 1.0, -1.0)
    sizes = jax.random.uniform(size_key, (KV_HEADS, D_HEAD), jnp.float32, 0.8, 1.2)
    channel = jax.random.randint(channel_key, (KV_HEADS,), 0, D_HEAD)
    strong = (jnp.arange(D_HEAD)[None, :] != channel[:, None]).astype(jnp.float32)
    pattern = signs * sizes * strong
    offset = jax.random.randint(offset_key, (), 0, CACHE_DEV)
    other = (offset + jax.random.randint(other_key, (), 1, CACHE_DEV)) % CACHE_DEV
    return (pattern, strong, offset, other)


def draw_keys(key, part):
    base = shared_keys(key)
    return base.astype(jnp.bfloat16)


def draw_queries(key, part):
    pattern, strong, offset, other = shared_pattern(key)
    key = jax.random.fold_in(key, 12)
    group_size = HEADS // KV_HEADS
    row_ids = jnp.arange(TOKENS)[:, None]
    fresh = 1.6 * jax.random.truncated_normal(key, -6.0, 6.0, (TOKENS, HEADS * D_HEAD), jnp.float32)
    planted = (76.0 * pattern[:, None, :] * jnp.ones((1, group_size, 1), jnp.float32)).reshape(HEADS * D_HEAD)
    fresh = jnp.where(row_ids % 97 == 7, planted[None, :], fresh)
    weak = (jnp.where(strong > 0.5, 1.0, 0.02)[:, None, :] * jnp.ones((1, group_size, 1), jnp.float32)).reshape(HEADS * D_HEAD)
    return (fresh * weak[None, :]).astype(jnp.bfloat16)


def draw_cache_keys(key, part):
    pattern, strong, offset, other = shared_pattern(key)
    key = jax.random.fold_in(key, 14)
    regular_key, copy_key, size_key, sign_key = jax.random.split(key, 4)
    regular = 1.6 * jax.random.truncated_normal(regular_key, -6.0, 6.0, (CACHE_TOK, KV_HEADS, D_HEAD), jnp.float32)
    copy_noise = 0.15 * jax.random.truncated_normal(copy_key, -4.0, 4.0, (CACHE_TOK, KV_HEADS, D_HEAD), jnp.float32)
    copies = (pattern[None, :, :] + copy_noise) * strong[None, :, :]
    outlier_sign = jnp.where(jax.random.bernoulli(sign_key, 0.5, (CACHE_TOK, KV_HEADS, 1)), 1.0, -1.0)
    outlier_size = jax.random.uniform(size_key, (CACHE_TOK, KV_HEADS, 1), jnp.float32, 90.0, 100.0)
    spiked = regular * strong[None, :, :] + outlier_sign * outlier_size * (1.0 - strong[None, :, :])
    row_in_page = (jnp.arange(CACHE_TOK) % CACHE_DEV)[:, None, None]
    result = jnp.where(row_in_page == offset, copies, jnp.where(row_in_page == other, spiked, regular))
    return result.reshape(CACHE_TOK, KV_HEADS * D_HEAD).astype(jnp.bfloat16)


def draw_window(key, part):
    key = jax.random.fold_in(key, 13)
    first_key, second_key = jax.random.split(key)
    base = jax.random.randint(first_key, (STRETCHES,), 1, CACHED + 1)
    chosen = jax.random.randint(second_key, (), 0, STRETCHES)
    return jnp.where(jnp.arange(STRETCHES) == chosen, CACHED, base).astype(jnp.int32)


def steps_of(own_key, dims, cuts, low, largest):
    loudness = 1.0
    for position, blocks in cuts:
        draws = jax.random.uniform(jax.random.fold_in(jax.random.fold_in(own_key, 6), position), (blocks,), jnp.float32, low / len(cuts), largest / len(cuts))
        loudness = loudness * jnp.repeat(jnp.exp(draws), dims[position] // blocks).reshape((-1,) + (1,) * (len(dims) - 1 - position))
    return loudness


def gaussian(stream_key, shape, scale, most, cuts=(), kind=jnp.bfloat16):
    gain = steps_of(stream_key, shape, cuts, -0.22, 0.18) if cuts else 1.0
    array = jax.random.normal(stream_key, shape, jnp.float32) * scale * gain
    return jnp.minimum(jnp.maximum(array, -most), most).astype(kind)


def setup_inputs(seed: int = 0) -> dict:
    streams_of = jax.random.split(jax.random.key(seed), 8)
    queries = draw_queries(jax.random.fold_in(streams_of[7], 71), 0)
    keys = draw_keys(jax.random.fold_in(streams_of[7], 71), 0)
    values = gaussian(streams_of[2], (TOKENS, KV_HEADS * D_HEAD), 1.0, 6.0, ((0, 64), (1, 4)))
    cache_keys = draw_cache_keys(jax.random.fold_in(streams_of[7], 71), 0)
    cache_values = gaussian(streams_of[4], (CACHE_TOK, KV_HEADS * D_HEAD), 1.0, 6.0, ((0, 256),))
    page_owner = jax.random.permutation(streams_of[5], PAGES).astype(jnp.int32)
    window = draw_window(jax.random.fold_in(streams_of[7], 71), 0)
    return dict(queries=queries, keys=keys, values=values, cache_keys=cache_keys, cache_values=cache_values, page_owner=page_owner, window=window)


neg_fill = -1e30


def reference(queries, keys, values, cache_keys, cache_values, page_owner, window):
    group_size = HEADS // KV_HEADS
    stretch_rows = TOKENS // STRETCHES
    slot_ids = jnp.arange(PAGES, dtype=jnp.int32)
    logical = jnp.zeros((PAGES,), jnp.int32).at[page_owner].set(slot_ids)
    cached_of_row = jnp.repeat(logical // (PAGES // CACHED), CACHE_DEV)
    fresh_of_row = jnp.arange(TOKENS, dtype=jnp.int32) // stretch_rows
    all_keys = jnp.concatenate([cache_keys, keys], 0).astype(jnp.float32).reshape(-1, KV_HEADS, D_HEAD)
    all_values = jnp.concatenate([cache_values, values], 0).astype(jnp.float32).reshape(-1, KV_HEADS, D_HEAD)

    def one_block(index):
        first_row = (index * TOK_DEV).astype(jnp.int32)
        query_block = lax.dynamic_slice_in_dim(queries, first_row, TOK_DEV, 0)
        query_block = query_block.astype(jnp.float32).reshape(TOK_DEV, KV_HEADS, group_size, D_HEAD)
        stretch_group = first_row // stretch_rows
        visible = jnp.concatenate([cached_of_row >= CACHED - window[stretch_group], fresh_of_row <= stretch_group])
        scores = jnp.einsum("qkgd,tkd->kgqt", query_block, all_keys) * (D_HEAD ** -0.5)
        scores = jnp.where(visible, scores, neg_fill)
        row_max = jnp.max(scores, axis=-1, keepdims=True)
        weights = jnp.where(visible, jnp.exp(scores - row_max), 0.0)
        rounded = lax.optimization_barrier(weights.astype(jnp.bfloat16)).astype(jnp.float32)
        summed = jnp.einsum("kgqt,tkd->qkgd", rounded, all_values)
        totals = jnp.transpose(jnp.sum(weights, axis=-1), (2, 0, 1))[..., None]
        return (summed / totals).reshape(TOK_DEV, HEADS * D_HEAD).astype(jnp.bfloat16)

    blocks = lax.map(one_block, jnp.arange(TOKENS // TOK_DEV, dtype=jnp.int32))
    return blocks.reshape(TOKENS, HEADS * D_HEAD)
```

```python
import functools

import jax
import jax.numpy as jnp
from jax import lax
from jax.experimental import pallas as pl
from jax.experimental.pallas import tpu as pltpu
from jax.sharding import Mesh, PartitionSpec as P

D = 128
GROUP = 6
WIDE = GROUP * D
HALF = 64
CROWS = 32
BLOCK = HALF + CROWS
ROWS = GROUP * HALF
NEG = -1e30
LOG2E = 1.4426950408889634
SCALE = D**-0.5 * LOG2E
KEYS = 512

VMEM = pltpu.VMEM
ANY = pl.ANY


def params(mib):
    return pltpu.CompilerParams(vmem_limit_bytes=mib * 2**20)


def slot():
    return 2 * (lax.axis_index("x") & 1) + lax.axis_index("core")


def cut_body(q_ref, k_ref, v_ref, ck_ref, cv_ref, *outs):
    q_out, kv_out, send_ref, own_ref = outs[:4], outs[4:8], outs[8], outs[9]
    x = lax.axis_index("x")
    half = lax.axis_index("zh")
    for s in range(4):
        piece = x ^ s
        rows = pl.ds(pl.multiple_of((piece & 1) * HALF, HALF), HALF)
        head = piece >> 1
        narrow = pl.ds(pl.multiple_of(head * D, D), D)
        kv_out[s][:, :D] = k_ref[rows, narrow]
        kv_out[s][:, D:] = v_ref[rows, narrow]
        q_out[s][...] = q_ref[rows, pl.ds(pl.multiple_of(head * WIDE, D), WIDE)]
    mine = pl.ds(pl.multiple_of(half * 4 * D, D), 4 * D)
    other = pl.ds(pl.multiple_of((1 - half) * 4 * D, D), 4 * D)
    own_ref[:, : 4 * D] = ck_ref[:, mine]
    own_ref[:, 4 * D :] = cv_ref[:, mine]
    send_ref[:, : 4 * D] = ck_ref[:, other]
    send_ref[:, 4 * D :] = cv_ref[:, other]


def cut(q, k, v, ck, cv):
    bf = jnp.bfloat16
    return pl.pallas_call(
        cut_body,
        out_shape=[jax.ShapeDtypeStruct((HALF, WIDE), bf)] * 4
        + [jax.ShapeDtypeStruct((HALF, 2 * D), bf)] * 4
        + [jax.ShapeDtypeStruct((16, 8 * D), bf)] * 2,
        name="cut",
    )(q, k, v, ck, cv)


def cut_cache_body(own_ref, got_ref, *outs):
    x = lax.axis_index("x")
    for s in range(4):
        head = (x + s) & 3
        for part, ref in enumerate((own_ref, got_ref)):
            rows = slice(16 * part, 16 * part + 16)
            outs[s][rows, :D] = ref[:, pl.ds(pl.multiple_of(head * D, D), D)]
            outs[s][rows, D:] = ref[:, pl.ds(pl.multiple_of((head + 4) * D, D), D)]


def cut_cache(own, got):
    return pl.pallas_call(
        cut_cache_body,
        out_shape=[jax.ShapeDtypeStruct((CROWS, 2 * D), jnp.bfloat16)] * 4,
        name="cut_cache",
    )(own, got)


def join_body(*refs):
    kv, cache, out = refs[:4], refs[4:8], refs[8]
    x = lax.axis_index("x")
    r = slot()
    for s in range(4):
        out[pl.ds(r ^ s, 1), :HALF, :] = kv[s][...][None]
        out[pl.ds((x + 4 - s) & 3, 1), HALF:, :] = cache[s][...][None]


def join(kv, cache):
    return pl.pallas_call(
        join_body,
        out_shape=jax.ShapeDtypeStruct((4, BLOCK, 2 * D), jnp.bfloat16),
        name="join",
    )(*kv, *cache)


def place_body(*refs):
    pieces, out = refs[:4], refs[4]
    x = lax.axis_index("x")
    for s in range(4):
        piece = x ^ s
        rows = pl.ds(pl.multiple_of((piece & 1) * HALF, HALF), HALF)
        out[rows, pl.ds(pl.multiple_of((piece >> 1) * WIDE, D), WIDE)] = pieces[s][...]


def place(pieces):
    return pl.pallas_call(
        place_body,
        out_shape=jax.ShapeDtypeStruct((2 * HALF, 2 * WIDE), jnp.bfloat16),
        name="place",
    )(*pieces)


def attend_body(owner_ref, window_ref, *refs):
    q_in, blocks, outs = refs[:4], refs[4:14], refs[14:18]
    fresh, paged, sorted_kv, q_all, acc, top, sem = refs[18:]
    r = slot()
    zl, y, core = lax.axis_index("zl"), lax.axis_index("y"), lax.axis_index("core")

    copies = []

    def bring(source, first, depth, ysrc, csrc):
        for i in range(depth):
            zsrc = (zl + 4 - (first + i)) & 3
            chip = zsrc * 4 + ysrc
            n = len(copies)
            one = pltpu.make_async_copy(
                source.at[i, :, :HALF, :],
                fresh.at[:, pl.ds(pl.multiple_of((chip * 2 + csrc) * HALF, HALF), HALF), :],
                sem.at[2 * n],
            )
            two = pltpu.make_async_copy(
                source.at[i, :, HALF:, :],
                paged.at[:, chip, pl.ds(pl.multiple_of(csrc * CROWS, CROWS), CROWS), :],
                sem.at[2 * n + 1],
            )
            one.start()
            two.start()
            copies.append((one, two))

    for which in range(2):
        c = core if which == 0 else 1 - core
        b = blocks[5 * which : 5 * which + 5]
        bring(b[0], 0, 4, y, c)
        bring(b[1], 0, 4, (y + 3) & 3, c)
        bring(b[2], 0, 4, (y + 1) & 3, c)
        bring(b[3], 0, 2, (y + 2) & 3, c)
        bring(b[4], 2, 2, (y + 2) & 3, c)

    for s in range(4):
        for g in range(GROUP):
            row = pl.multiple_of((r ^ s) * ROWS + g * HALF, HALF)
            q_all[pl.ds(row, HALF), :] = q_in[s][:, g * D : (g + 1) * D]
    acc[...] = jnp.zeros_like(acc)
    top[...] = jnp.full_like(top, NEG)
    for one, two in copies:
        one.wait()
        two.wait()

    ones = jnp.ones((KEYS, D), jnp.bfloat16)

    def step(c, kv):
        rows = slice(c * ROWS, (c + 1) * ROWS)
        k = kv[:, :D]
        v = jnp.concatenate([kv[:, D:], ones], axis=1)
        s = lax.dot_general(
            q_all[rows, :], k, (((1,), (1,)), ((), ())), preferred_element_type=jnp.float32
        )
        old = top[rows, :]
        new = jnp.maximum(old, jnp.max(s, axis=1, keepdims=True))
        p = jnp.exp2((s - new[:, :1]) * SCALE).astype(jnp.bfloat16)
        update = lax.dot_general(
            p, v, (((1,), (0,)), ((), ())), preferred_element_type=jnp.float32
        )
        factor = jnp.exp2((old - new) * SCALE)
        acc[rows, :D] = acc[rows, :D] * factor + update[:, :D]
        acc[rows, D:] = acc[rows, D:] * factor + update[:, D:]
        top[rows, :] = new

    for t in range(4):

        def fresh_step(i, carry, t=t):
            kv = fresh[t, pl.ds(pl.multiple_of(i * KEYS, KEYS), KEYS), :]
            for c in range(t, 4):
                step(c, kv)
            return carry

        lax.fori_loop(0, 2048 // KEYS, fresh_step, 0)

    pages = KEYS // 64
    for cached in range(2):

        def sort_step(i, carry, cached=cached):
            page = owner_ref[cached * 32 + i]
            sorted_kv[pl.ds(pl.multiple_of(i * 64, 64), 64), :] = paged[page >> 4, page & 15]
            return carry

        lax.fori_loop(0, 32, sort_step, 0)

        def cache_step(i, carry, c):
            step(c, sorted_kv[pl.ds(pl.multiple_of(i * KEYS, KEYS), KEYS), :])
            return carry

        for c in range(4):
            if cached == 1:
                lax.fori_loop(0, 2048 // KEYS, functools.partial(cache_step, c=c), 0)
            else:

                @pl.when(window_ref[c] > 1)
                def _(c=c):
                    lax.fori_loop(0, 2048 // KEYS, functools.partial(cache_step, c=c), 0)

    for s in range(4):
        for g in range(GROUP):
            row = pl.multiple_of((r ^ s) * ROWS + g * HALF, HALF)
            total = acc[pl.ds(row, HALF), :]
            outs[s][:, g * D : (g + 1) * D] = (total[:, :D] / total[:, D:]).astype(jnp.bfloat16)


def attend(owner, window, q, blocks):
    bf = jnp.bfloat16
    smem = pl.BlockSpec(memory_space=pltpu.SMEM)
    vmem = pl.BlockSpec(memory_space=VMEM)
    return pl.pallas_call(
        attend_body,
        in_specs=[smem, smem] + [vmem] * 4 + [pl.BlockSpec(memory_space=ANY)] * 10,
        out_specs=[vmem] * 4,
        out_shape=[jax.ShapeDtypeStruct((HALF, WIDE), bf)] * 4,
        scratch_shapes=[
            VMEM((4, 2048, 2 * D), bf),
            VMEM((4, 16, 64, 2 * D), bf),
            VMEM((2048, 2 * D), bf),
            VMEM((4 * ROWS, D), bf),
            VMEM((4 * ROWS, 2 * D), jnp.float32),
            VMEM((4 * ROWS, D), jnp.float32),
            pltpu.SemaphoreType.DMA((64,)),
        ],
        compiler_params=params(48),
        name="attend",
    )(owner, window, *q, *blocks)


def spread(s):
    pairs = []
    for x in range(4):
        for core in range(2):
            piece = x ^ s
            pairs.append((x * 2 + core, (2 * core + (piece >> 1)) * 2 + (piece & 1)))
    return pairs


def shift(array, axis, by, size=4):
    return lax.ppermute(array, axis, [(i, (i + by) % size) for i in range(size)])


def on_device(queries, keys, values, cache_keys, cache_values, page_owner, window):
    made = cut(queries, keys, values, cache_keys, cache_values)
    q_pieces, kv_pieces, send, own = made[:4], made[4:8], made[8], made[9]
    got = shift(send, "zh", 1, 2)
    kv = [lax.ppermute(kv_pieces[s], ("x", "core"), spread(s)) for s in range(4)]
    q = [lax.ppermute(q_pieces[s], ("x", "core"), spread(s)) for s in range(4)]
    cache_pieces = cut_cache(own, got)
    cache = [cache_pieces[0]] + [shift(cache_pieces[s], "x", s) for s in range(1, 4)]
    block = join(kv, cache)
    column = jnp.stack([block] + [shift(block, "zl", s) for s in range(1, 4)])
    up = shift(column, "y", 1)
    down = shift(column, "y", 3)
    far_a = shift(up[:2], "y", 1)
    far_b = shift(down[2:], "y", 3)
    mine = [column, up, down, far_a, far_b]
    theirs = [shift(part, "core", 1, 2) for part in mine]
    outs = attend(page_owner, window, q, mine + theirs)
    back = [
        lax.ppermute(outs[s], ("x", "core"), [(b, a) for a, b in spread(s)]) for s in range(4)
    ]
    return place(back)


def solution(mesh):
    fine = Mesh(mesh.devices.reshape(4, 4, 4, 2, 2), ("x", "zl", "y", "zh", "core"))
    tokens, heads = ("x", "zl", "y"), ("zh", "core")
    return jax.shard_map(
        on_device,
        mesh=fine,
        in_specs=(
            P(tokens, heads),
            P(tokens, heads),
            P(tokens, heads),
            P(tokens + heads, None),
            P(tokens + heads, None),
            P(),
            P(),
        ),
        out_specs=P(tokens, heads),
        check_vma=False,
    )
```

```python
import jax
import jax.numpy as jnp
from jax import lax
from jax.experimental import pallas as pl
from jax.experimental.pallas import tpu as pltpu
from jax.sharding import Mesh, PartitionSpec as P

D = 128
GROUP = 6
WIDE = GROUP * D
HALF = 64
CROWS = 32
BLOCK = HALF + CROWS
ROWS = GROUP * HALF
NEG = -1e30
SCALE = D**-0.5 * 1.4426950408889634

VMEM = pltpu.VMEM
BF = jnp.bfloat16
F32 = jnp.float32
vmem = pl.BlockSpec(memory_space=VMEM)
smem = pl.BlockSpec(memory_space=pltpu.SMEM)


def shaped(shape, dtype=BF):
    return jax.ShapeDtypeStruct(shape, dtype)


def slot():
    return 2 * (lax.axis_index("x") & 1) + lax.axis_index("core")


def aligned(index, step):
    return pl.ds(pl.multiple_of(index * step, step), step)


def cut_body(q_ref, k_ref, v_ref, ck_ref, cv_ref, core_ref, half_ref):
    other = aligned(1 - lax.axis_index("core"), HALF)
    core_ref[:, : 2 * D] = k_ref[other, :]
    core_ref[:, 2 * D : 4 * D] = v_ref[other, :]
    core_ref[:, 4 * D :] = q_ref[other, :]
    lanes = aligned(1 - lax.axis_index("zh"), 4 * D)
    half_ref[:, : 4 * D] = ck_ref[:, lanes]
    half_ref[:, 4 * D :] = cv_ref[:, lanes]


def cut(q, k, v, ck, cv):
    return pl.pallas_call(
        cut_body,
        out_shape=[shaped((HALF, 4 * D + 2 * WIDE)), shaped((16, 8 * D))],
        name="cut",
    )(q, k, v, ck, cv)


def deal_body(k_ref, v_ref, ck_ref, cv_ref, core_ref, half_ref, out):
    core = lax.axis_index("core")
    rows = aligned(core, HALF)
    lanes = aligned(lax.axis_index("zh"), 4 * D)
    mine_k, mine_v = ck_ref[:, lanes], cv_ref[:, lanes]
    for e in range(2):
        lane = slice(e * D, (e + 1) * D)
        later = slice((2 + e) * D, (3 + e) * D)
        own, got = pl.ds(2 * core + e, 1), pl.ds(2 * (1 - core) + e, 1)
        out[own, :HALF, :D] = k_ref[rows, lane][None]
        out[own, :HALF, D:] = v_ref[rows, lane][None]
        out[got, :HALF, :D] = core_ref[:, lane][None]
        out[got, :HALF, D:] = core_ref[:, later][None]
    for h in range(4):
        lane = slice(h * D, (h + 1) * D)
        out[h, HALF : HALF + 16, :D] = mine_k[:, lane]
        out[h, HALF : HALF + 16, D:] = mine_v[:, lane]
        out[h, HALF + 16 :, :D] = half_ref[:, lane]
        out[h, HALF + 16 :, D:] = half_ref[:, (4 + h) * D : (5 + h) * D]


def deal(k, v, ck, cv, from_core, from_half):
    return pl.pallas_call(
        deal_body, out_shape=shaped((4, BLOCK, 2 * D)), name="deal"
    )(k, v, ck, cv, from_core, from_half)


def deal_q_body(q_ref, core_ref, out):
    core = lax.axis_index("core")
    rows = aligned(core, HALF)
    for e in range(2):
        out[pl.ds(2 * core + e, 1)] = q_ref[rows, e * WIDE : (e + 1) * WIDE][None]
        lanes = slice(4 * D + e * WIDE, 4 * D + (e + 1) * WIDE)
        out[pl.ds(2 * (1 - core) + e, 1)] = core_ref[:, lanes][None]


def deal_q(q, from_core):
    return pl.pallas_call(deal_q_body, out_shape=shaped((4, HALF, WIDE)), name="deal_q")(
        q, from_core
    )


def join_q_body(ref, out):
    for c in range(4):
        for g in range(GROUP):
            out[c, g * HALF : (g + 1) * HALF, :] = ref[c, :, g * D : (g + 1) * D]


def join_q(pieces):
    return pl.pallas_call(join_q_body, out_shape=shaped((4, ROWS, D)), name="join_q")(pieces)


def place_body(*refs):
    x = lax.axis_index("x")
    for s in range(4):
        piece = x ^ s
        refs[4][aligned(piece & 1, HALF), aligned(piece >> 1, WIDE)] = refs[s][...]


def place(pieces):
    return pl.pallas_call(
        place_body, out_shape=shaped((2 * HALF, 2 * WIDE)), name="place"
    )(*pieces)


def absorb(q, k, v, bias, state, c):
    s = lax.dot_general(q, k, (((1,), (1,)), ((), ())), preferred_element_type=F32)
    paged = bias.shape[1]
    s = jnp.concatenate([s[:, :paged] + bias, s[:, paged:]], axis=1)
    new = jnp.max(s, axis=1, keepdims=True)
    if state is None:
        new = jnp.broadcast_to(new, (s.shape[0], D))
    else:
        acc, top = state
        old = top[c]
        new = jnp.maximum(old, new)
    p = jnp.exp2((s - new[:, :1]) * SCALE).astype(BF)
    update = lax.dot_general(p, v, (((1,), (0,)), ((), ())), preferred_element_type=F32)
    out, norm = update[:, :D], update[:, D:]
    if state is not None:
        factor = jnp.exp2((old - new) * SCALE)
        out, norm = acc[c, :, :D] * factor + out, acc[c, :, D:] * factor + norm
    return out, norm, new


def attend_body(halves, first, last, refs):
    refs = list(refs)
    take = lambda n: [refs.pop(0) for _ in range(n)]
    window_ref, bias_ref = take(2)
    q_refs = take(halves)
    states = [None if first else take(2) for _ in range(halves)]
    keys, vals = refs.pop(-2), refs.pop(-1)
    outs = [refs.pop(-1) for _ in range(2 * halves)][::-1]
    blocks = refs
    total = keys.shape[0]
    at = 0
    for t in range(-4, 4):
        for block in blocks:
            part = block[t + 4, HALF:, :] if t < 0 else block[t, :HALF, :]
            depth = part.shape[0]
            keys[at : at + depth, :] = part[:, :D]
            vals[at : at + depth, :D] = part[:, D:]
            at += depth
    vals[:, D:] = jnp.ones((total, D), BF)
    paged = 4 * CROWS * len(blocks)
    for c in range(4):
        n = paged + (c + 1) * HALF * len(blocks)
        bias = jnp.where(window_ref[c] > 1, 0.0, bias_ref[...])
        for h in range(halves):
            out, norm, new = absorb(q_refs[h][c], keys[:n, :], vals[:n, :], bias, states[h], c)
            one, two = outs[2 * h], outs[2 * h + 1]
            if last:
                one[c] = (out / norm).astype(BF)
                two[c] = (new * SCALE + jnp.log2(norm)).T[:8]
            else:
                one[c, :, :D] = out
                one[c, :, D:] = norm
                two[c] = new


def attend(q, state, blocks, window, bias, last=False):
    halves = len(q)
    total = BLOCK * 4 * len(blocks)
    kept = [] if state is None else list(state)
    work = halves * 4 * ROWS * len(blocks) * (4 * CROWS + 2.5 * HALF)
    if last:
        shapes = [shaped((4, ROWS, D)), shaped((4, 8, ROWS), F32)]
    else:
        shapes = [shaped((4, ROWS, 2 * D), F32), shaped((4, ROWS, D), F32)]
    return pl.pallas_call(
        lambda *refs: attend_body(halves, state is None, last, refs),
        in_specs=[smem] + [vmem] * (1 + halves + len(kept) + len(blocks)),
        out_specs=[vmem] * (2 * halves),
        out_shape=shapes * halves,
        scratch_shapes=[VMEM((total, D), BF), VMEM((total, 2 * D), BF)],
        compiler_params=pltpu.CompilerParams(vmem_limit_bytes=40 * 2**20),
        cost_estimate=pl.CostEstimate(
            flops=int(work * D * 4 * 2), bytes_accessed=2**20, transcendentals=int(work)
        ),
        name="attend",
    )(window, bias, *q, *kept, *blocks)


def merge_body(acc, top, got_ref, log_ref, *outs):
    r = slot()
    for s in range(4):
        c = r ^ s
        norm = acc[c, :, D:]
        mine = top[c] * SCALE + jnp.log2(norm)
        theirs = jnp.broadcast_to(log_ref[c][:1], (D, ROWS)).T
        most = jnp.maximum(mine, theirs)
        one, two = jnp.exp2(mine - most), jnp.exp2(theirs - most)
        both = (acc[c, :, :D] / norm * one + got_ref[c].astype(F32) * two) / (one + two)
        for g in range(GROUP):
            outs[s][:, g * D : (g + 1) * D] = both[g * HALF : (g + 1) * HALF, :].astype(BF)


def merge(acc, top, got, log):
    return pl.pallas_call(
        merge_body, out_shape=[shaped((HALF, WIDE))] * 4, name="merge"
    )(acc, top, got, log)


def spread(s):
    pairs = []
    for x in range(4):
        for core in range(2):
            piece = x ^ s
            pairs.append((x * 2 + core, (2 * core + (piece >> 1)) * 2 + (piece & 1)))
    return pairs


def shift(array, axis, by, size=4):
    return lax.ppermute(array, axis, [(i, (i + by) % size) for i in range(size)])


def swap(array):
    return shift(array, "core", 1, 2)


RING = (0, 2, 3, 1)


def loop_pairs(axis_of_core):
    pairs = []
    for zl in range(4):
        for y in range(4):
            for core in range(2):
                z2, y2 = zl, y
                if axis_of_core[core] == "y":
                    y2 = (y + 1) % 4
                else:
                    z2 = RING[(RING.index(zl) + 1) % 4]
                pairs.append(((zl * 4 + y) * 2 + core, (z2 * 4 + y2) * 2 + core))
    return pairs


def step_on(block, phase):
    pairs = loop_pairs(("zl", "y") if phase == 0 else ("y", "zl"))
    return lax.ppermute(block, ("zl", "y", "core"), pairs)


def cache_bias(page_owner):
    zl, y, core = lax.axis_index("zl"), lax.axis_index("y"), lax.axis_index("core")
    shape = (4, 4, 4, CROWS)
    b = lax.broadcasted_iota(jnp.int32, shape, 0)
    xs = lax.broadcasted_iota(jnp.int32, shape, 1)
    a = lax.broadcasted_iota(jnp.int32, shape, 2)
    z_steps, y_steps = jnp.where(core == 0, a, b), jnp.where(core == 0, b, a)
    index = jnp.where(zl == 0, 0, jnp.where(zl == 2, 1, jnp.where(zl == 3, 2, 3)))
    at = (index + 4 - z_steps) & 3
    zs = jnp.where(at == 0, 0, jnp.where(at == 1, 2, jnp.where(at == 2, 3, 1)))
    page = (xs * 4 + zs) * 4 + ((y + 4 - y_steps) & 3)
    page = page.reshape(4, 1, -1, 1)
    late = jnp.any(page == page_owner[None, None, None, 32:], axis=3)
    return jnp.where(late, 0.0, NEG).astype(F32)


def on_device(queries, keys, values, cache_keys, cache_values, page_owner, window):
    to_core, to_half = cut(queries, keys, values, cache_keys, cache_values)
    from_core, from_half = swap(to_core), shift(to_half, "zh", 1, 2)
    heads = deal(keys, values, cache_keys, cache_values, from_core, from_half)
    block = lax.all_to_all(heads, "x", split_axis=0, concat_axis=0, tiled=True)
    row = [block]
    for _ in range(3):
        row.append(step_on(row[-1], 0))
    q = lax.all_to_all(
        deal_q(queries, from_core), "x", split_axis=0, concat_axis=0, tiled=True
    )
    mine = join_q(q)
    theirs = swap(mine)
    bias = cache_bias(page_owner)

    state = None
    for b in range(4):
        if b == 3:
            break
        following = [step_on(one, 1) for one in row]
        state = attend([theirs, mine], state, row, window, bias[b])
        row = following
    out, log = attend([theirs], state[:2], row, window, bias[3], last=True)
    out, log = swap(out), swap(log)
    kept = attend([mine], state[2:], row, window, bias[3])
    pieces = merge(*kept, out, log)
    back = [
        lax.ppermute(pieces[s], ("x", "core"), [(b, a) for a, b in spread(s)]) for s in range(4)
    ]
    return place(back)


def solution(mesh):
    fine = Mesh(mesh.devices.reshape(4, 4, 4, 2, 2), ("x", "zl", "y", "zh", "core"))
    tokens, heads = ("x", "zl", "y"), ("zh", "core")
    return jax.shard_map(
        on_device,
        mesh=fine,
        in_specs=(
            P(tokens, heads),
            P(tokens, heads),
            P(tokens, heads),
            P(tokens + heads, None),
            P(tokens + heads, None),
            P(),
            P(),
        ),
        out_specs=P(tokens, heads),
        check_vma=False,
    )
```

```python
import jax
import jax.numpy as jnp
from jax import lax
from jax.experimental import pallas as pl
from jax.experimental.pallas import tpu as pltpu
from jax.sharding import Mesh, PartitionSpec as P

D = 128
GROUP = 6
WIDE = GROUP * D
HALF = 64
CROWS = 32
BLOCK = HALF + CROWS
ROWS = GROUP * HALF
NEG = -1e30
SCALE = D**-0.5 * 1.4426950408889634

VMEM = pltpu.VMEM
BF = jnp.bfloat16
F32 = jnp.float32
vmem = pl.BlockSpec(memory_space=VMEM)
smem = pl.BlockSpec(memory_space=pltpu.SMEM)


def shaped(shape, dtype=BF):
    return jax.ShapeDtypeStruct(shape, dtype)


def slot():
    return 2 * (lax.axis_index("x") & 1) + lax.axis_index("core")


def aligned(index, step):
    return pl.ds(pl.multiple_of(index * step, step), step)


def deal_body(q_ref, k_ref, v_ref, ck_ref, cv_ref, q_got, k_got, v_got, c_got, *outs):
    x, half, core = lax.axis_index("x"), lax.axis_index("zh"), lax.axis_index("core")
    rows = aligned(core, HALF)
    for s in range(4):
        head = (x + s) & 3
        out, q_out = outs[s], outs[4 + s]

        def from_core(q, k, v, out=out, q_out=q_out, e=head & 1):
            out[:HALF, :D] = k[rows, aligned(e, D)]
            out[:HALF, D:] = v[rows, aligned(e, D)]
            for i in range(3):
                lanes = pl.ds(pl.multiple_of(e * WIDE + i * 2 * D, D), 2 * D)
                q_out[i * HALF : (i + 1) * HALF, :] = q[rows, lanes]

        @pl.when((head >> 1) == core)
        def _():
            from_core(q_ref, k_ref, v_ref)

        @pl.when((head >> 1) != core)
        def _():
            from_core(q_got, k_got, v_got)

        lanes = aligned(half * 4 + head, D)
        out[HALF : HALF + 16, :D] = ck_ref[:, lanes]
        out[HALF : HALF + 16, D:] = cv_ref[:, lanes]
        lanes = aligned(head, D)
        out[HALF + 16 : BLOCK, :D] = c_got[:16, lanes]
        out[HALF + 16 : BLOCK, D:] = c_got[16:, lanes]


def deal(own, got):
    return pl.pallas_call(
        deal_body,
        out_shape=[shaped((BLOCK, 2 * D))] * 4 + [shaped((3 * HALF, 2 * D))] * 4,
        name="deal",
    )(*own, *got)


def join_body(*refs):
    x = lax.axis_index("x")
    for s in range(4):
        refs[4][pl.ds((x + 4 - s) & 3, 1)] = refs[s][...][None]


def join(messages):
    return pl.pallas_call(
        join_body, out_shape=shaped((4, *messages[0].shape)), name="join"
    )(*messages)


def attend_body(first, last, refs):
    refs = list(refs)
    take = lambda n: [refs.pop(0) for _ in range(n)]
    window_ref, bias_ref = take(2)
    q_refs = take(2)
    states = [None if first else take(2) for _ in range(2)]
    scratch = [refs.pop(-1) for _ in range(3 if last else 2)][::-1]
    keys, vals = scratch[:2]
    outs = [refs.pop(-1) for _ in range(4)][::-1]
    blocks = refs
    total = keys.shape[0]
    at = 0
    for t in range(-4, 4):
        for block in blocks:
            part = block[t + 4, HALF:, :] if t < 0 else block[t, :HALF, :]
            depth = part.shape[0]
            keys[at : at + depth, :] = part[:, :D]
            vals[at : at + depth, :D] = part[:, D:]
            at += depth
    vals[:, D:] = jnp.ones((total, D), BF)
    paged = 4 * CROWS * len(blocks)
    core = lax.axis_index("core")
    lane = lax.broadcasted_iota(jnp.int32, (HALF, D), 1)

    def seen(c):
        return paged + (c + 1) * HALF * len(blocks)

    def scores(h, c):
        q = [
            q_refs[h][c, g // 2 * HALF : (g // 2 + 1) * HALF, g % 2 * D : (g % 2 + 1) * D]
            for g in range(GROUP)
        ]
        s = lax.dot_general(
            jnp.concatenate(q, axis=0),
            keys[: seen(c), :],
            (((1,), (1,)), ((), ())),
            preferred_element_type=F32,
        )
        bias = jnp.where(window_ref[c] > 1, 0.0, bias_ref[...])
        return jnp.concatenate([s[:, :paged] + bias, s[:, paged:]], axis=1)

    def absorb(h, c, s):
        new = jnp.max(s, axis=1, keepdims=True)
        if first:
            new = jnp.broadcast_to(new, (ROWS, D))
        else:
            acc, top = states[h]
            old = top[c]
            new = jnp.maximum(old, new)
        p = jnp.exp2((s - new[:, :1]) * SCALE).astype(BF)
        update = jnp.dot(p, vals[: seen(c), :], preferred_element_type=F32)
        out, norm = update[:, :D], update[:, D:]
        if not first:
            factor = jnp.exp2((old - new) * SCALE)
            out, norm = acc[c, :, :D] * factor + out, acc[c, :, D:] * factor + norm
        if not last:
            outs[2 * h][c, :, :D] = out
            outs[2 * h][c, :, D:] = norm
            outs[2 * h + 1][c] = new
            return
        out = (out / norm).astype(BF)
        log = new * SCALE + jnp.log2(norm)
        made = scratch[2]
        rows = aligned(core if h == 0 else 1 - core, HALF)
        logs = jnp.zeros((HALF, D), F32)
        for g in range(GROUP):
            part = slice(g * HALF, (g + 1) * HALF)
            made[c, rows, g * D : (g + 1) * D] = out[part, :]
            left = log[part, :]
            for i in range(3):
                term = left.astype(BF).astype(F32)
                logs = jnp.where(lane == 3 * g + i, term, logs)
                left = left - term
        made[c, rows, WIDE:] = logs.astype(BF)

    steps = [(h, c) for c in range(4) for h in range(2)]
    ahead = scores(*steps[0])
    for n, step in enumerate(steps):
        now, ahead = ahead, scores(*steps[n + 1]) if n + 1 < len(steps) else None
        absorb(*step, now)
    if last:
        r = slot()
        for s in range(4):
            outs[s][...] = scratch[2][r ^ s]


def attend(q, state, blocks, window, bias, last=False):
    total = BLOCK * 4 * len(blocks)
    kept = [] if state is None else list(state)
    work = 8 * ROWS * len(blocks) * (4 * CROWS + 2.5 * HALF)
    if last:
        shapes = [shaped((2 * HALF, WIDE + D))] * 4
    else:
        shapes = [shaped((4, ROWS, 2 * D), F32), shaped((4, ROWS, D), F32)] * 2
    return pl.pallas_call(
        lambda *refs: attend_body(state is None, last, refs),
        in_specs=[smem] + [vmem] * (3 + len(kept) + len(blocks)),
        out_specs=[vmem] * 4,
        out_shape=shapes,
        scratch_shapes=[VMEM((total, D), BF), VMEM((total, 2 * D), BF)]
        + ([VMEM((4, 2 * HALF, WIDE + D), BF)] if last else []),
        compiler_params=pltpu.CompilerParams(vmem_limit_bytes=40 * 2**20),
        cost_estimate=pl.CostEstimate(
            flops=int(work * D * 4 * 2), bytes_accessed=2**20, transcendentals=int(work)
        ),
        name="attend",
    )(window, bias, *q, *kept, *blocks)


def merge_body(*refs):
    out = refs[4]
    x = lax.axis_index("x")
    lane = lax.broadcasted_iota(jnp.int32, (D, WIDE), 0)
    head = lax.broadcasted_iota(jnp.int32, (D, WIDE), 1) // D
    pick = jnp.where((lane // 3 == head) & (lane < 3 * GROUP), 1.0, 0.0).astype(BF)
    for pair in range(2):
        one, two = refs[2 * pair], refs[2 * pair + 1]
        a, b = (jnp.dot(ref[:, WIDE:], pick, preferred_element_type=F32) for ref in (one, two))
        most = jnp.maximum(a, b)
        a, b = jnp.exp2(a - most), jnp.exp2(b - most)
        both = (one[:, :WIDE].astype(F32) * a + two[:, :WIDE].astype(F32) * b) / (a + b)
        out[:, aligned((x >> 1) ^ pair, WIDE)] = both.astype(BF)


def merge(messages):
    return pl.pallas_call(
        merge_body, out_shape=shaped((2 * HALF, 2 * WIDE)), name="merge"
    )(*messages)


def spread(s):
    pairs = []
    for x in range(4):
        for core in range(2):
            piece = x ^ s
            pairs.append((x * 2 + core, (2 * core + (piece >> 1)) * 2 + (piece & 1)))
    return pairs


def shift(array, axis, by, size=4):
    return lax.ppermute(array, axis, [(i, (i + by) % size) for i in range(size)])


def swap(array):
    return shift(array, "core", 1, 2)


RING = (0, 2, 3, 1)


def loop_pairs(axis_of_core, by):
    pairs = []
    for zl in range(4):
        for y in range(4):
            for core in range(2):
                z2, y2 = zl, y
                if axis_of_core[core] == "y":
                    y2 = (y + by) % 4
                else:
                    z2 = RING[(RING.index(zl) + by) % 4]
                pairs.append(((zl * 4 + y) * 2 + core, (z2 * 4 + y2) * 2 + core))
    return pairs


def step_on(block, phase, by=1):
    pairs = loop_pairs(("zl", "y") if phase == 0 else ("y", "zl"), by)
    return lax.ppermute(block, ("zl", "y", "core"), pairs)


def cache_bias(page_owner, blocks):
    zl, y, core = lax.axis_index("zl"), lax.axis_index("y"), lax.axis_index("core")
    shape = (4, len(blocks), CROWS)
    xs = lax.broadcasted_iota(jnp.int32, shape, 0)
    n = lax.broadcasted_iota(jnp.int32, shape, 1)
    a = b = jnp.zeros(shape, jnp.int32)
    for i, (a_steps, b_steps) in enumerate(blocks):
        a, b = jnp.where(n == i, a_steps, a), jnp.where(n == i, b_steps, b)
    z_steps, y_steps = jnp.where(core == 0, a, b), jnp.where(core == 0, b, a)
    index = jnp.where(zl == 0, 0, jnp.where(zl == 2, 1, jnp.where(zl == 3, 2, 3)))
    at = (index + 4 - z_steps) & 3
    zs = jnp.where(at == 0, 0, jnp.where(at == 1, 2, jnp.where(at == 2, 3, 1)))
    page = (xs * 4 + zs) * 4 + ((y + 4 - y_steps) & 3)
    page = page.reshape(1, -1, 1)
    late = jnp.any(page == page_owner[None, None, 32:], axis=2)
    return jnp.where(late, 0.0, NEG).astype(F32)


PIECES = (
    ((0, 0), (1, 0)),
    ((3, 0), (0, 1), (1, 1), (2, 0)),
    ((3, 1), (0, 2), (2, 1), (1, 2)),
    ((3, 2), (0, 3), (1, 3), (3, 3)),
    ((2, 2), (2, 3)),
)
MOVES = (
    ((0, 1), (1, 1), (3, 1), (0, 2)),
    ((2, 1), (1, 2), (3, 2), (0, 3)),
    ((2, 2), (1, 3), (3, 3)),
    ((2, 3),),
    (),
)


def on_device(queries, keys, values, cache_keys, cache_values, page_owner, window):
    got = [swap(one) for one in (queries, keys, values)]
    start = 4 * D * (1 - lax.axis_index("zh"))
    halves = [lax.dynamic_slice_in_dim(c, start, 4 * D, 1) for c in (cache_keys, cache_values)]
    got.append(shift(jnp.concatenate(halves), "zh", 1, 2))
    messages = list(deal((queries, keys, values, cache_keys, cache_values), got))
    for s in (1, 3, 2):
        messages[s] = shift(messages[s], "x", s)
        messages[4 + s] = shift(messages[4 + s], "x", s)
    block = join(messages[:4])
    mine = join(messages[4:])
    q = [mine, swap(mine)]
    blocks = {(0, 0): block}
    blocks[1, 0] = step_on(block, 0)
    blocks[3, 0] = step_on(block, 0, 3)
    blocks[2, 0] = step_on(blocks[1, 0], 0)
    state = None
    for piece, moves in zip(PIECES, MOVES):
        for a, b in moves:
            before = blocks[a, b - 1]
            if state is not None:
                before, *state = lax.optimization_barrier((before, *state))
            blocks[a, b] = step_on(before, 1)
        state = attend(
            q,
            state,
            [blocks[one] for one in piece],
            window,
            cache_bias(page_owner, piece),
            last=piece is PIECES[-1],
        )
    back = [
        lax.ppermute(state[s], ("x", "core"), [(b, a) for a, b in spread(s)]) for s in range(4)
    ]
    return merge(back)


def solution(mesh):
    fine = Mesh(mesh.devices.reshape(4, 4, 4, 2, 2), ("x", "zl", "y", "zh", "core"))
    tokens, heads = ("x", "zl", "y"), ("zh", "core")
    return jax.shard_map(
        on_device,
        mesh=fine,
        in_specs=(
            P(tokens, heads),
            P(tokens, heads),
            P(tokens, heads),
            P(tokens + heads, None),
            P(tokens + heads, None),
            P(),
            P(),
        ),
        out_specs=P(tokens, heads),
        check_vma=False,
    )
```

```python
import jax
import jax.numpy as jnp
from jax import lax
from jax.experimental import pallas as pl
from jax.experimental.pallas import tpu as pltpu
from jax.sharding import Mesh, PartitionSpec as P

D = 128
GROUP = 6
WIDE = GROUP * D
HALF = 64
CROWS = 32
BLOCK = HALF + CROWS
MESSAGE = BLOCK + 3 * HALF
ROWS = GROUP * HALF
NEG = -1e30
SCALE = D**-0.5 * 1.4426950408889634

VMEM = pltpu.VMEM
BF = jnp.bfloat16
F32 = jnp.float32
vmem = pl.BlockSpec(memory_space=VMEM)
smem = pl.BlockSpec(memory_space=pltpu.SMEM)


def shaped(shape, dtype=BF):
    return jax.ShapeDtypeStruct(shape, dtype)


def slot():
    return 2 * (lax.axis_index("x") & 1) + lax.axis_index("core")


def aligned(index, step):
    return pl.ds(pl.multiple_of(index * step, step), step)


def deal_body(q_ref, k_ref, v_ref, ck_ref, cv_ref, q_got, k_got, v_got, c_got, *outs):
    x, half, core = lax.axis_index("x"), lax.axis_index("zh"), lax.axis_index("core")
    rows = aligned(core, HALF)
    for s in range(4):
        head = (x + s) & 3
        out = outs[s]

        def from_core(q, k, v, out=out, e=head & 1):
            out[:HALF, :D] = k[rows, aligned(e, D)]
            out[:HALF, D:] = v[rows, aligned(e, D)]
            for i in range(3):
                lanes = pl.ds(pl.multiple_of(e * WIDE + i * 2 * D, D), 2 * D)
                out[BLOCK + i * HALF : BLOCK + (i + 1) * HALF, :] = q[rows, lanes]

        @pl.when((head >> 1) == core)
        def _():
            from_core(q_ref, k_ref, v_ref)

        @pl.when((head >> 1) != core)
        def _():
            from_core(q_got, k_got, v_got)

        lanes = aligned(half * 4 + head, D)
        out[HALF : HALF + 16, :D] = ck_ref[:, lanes]
        out[HALF : HALF + 16, D:] = cv_ref[:, lanes]
        lanes = aligned(head, D)
        out[HALF + 16 : BLOCK, :D] = c_got[:16, lanes]
        out[HALF + 16 : BLOCK, D:] = c_got[16:, lanes]


def deal(own, got):
    return pl.pallas_call(
        deal_body, out_shape=[shaped((MESSAGE, 2 * D))] * 4, name="deal"
    )(*own, *got)


def join_body(*refs):
    x = lax.axis_index("x")
    block, q = refs[4:]
    for s in range(4):
        source = pl.ds((x + 4 - s) & 3, 1)
        block[source] = refs[s][:BLOCK, :][None]
        q[source] = refs[s][BLOCK:, :][None]


def join(messages):
    return pl.pallas_call(
        join_body,
        out_shape=[shaped((4, BLOCK, 2 * D)), shaped((4, 3 * HALF, 2 * D))],
        name="join",
    )(*messages)


def attend_body(first, last, refs):
    window_ref, bias_ref, *refs = refs
    q_refs, refs = refs[:2], refs[2:]
    if not first:
        acc, top, *refs = refs
    q_all, keys, vals, *made = refs[-4:] if last else refs[-3:]
    blocks, outs = (refs[:-8], refs[-8:-4]) if last else (refs[:-5], refs[-5:-3])
    blocks = [pair.at[i] for pair in blocks for i in range(2)]
    total = keys.shape[0]
    for h in range(2):
        for c in range(4):
            for g in range(GROUP):
                rows = slice(g // 2 * HALF, (g // 2 + 1) * HALF)
                part = q_refs[h][c, rows, g % 2 * D : (g % 2 + 1) * D]
                q_all[h, c, g * HALF : (g + 1) * HALF, :] = part
    at = 0
    for t in range(-4, 4):
        for block in blocks:
            part = block[t + 4, HALF:, :] if t < 0 else block[t, :HALF, :]
            depth = part.shape[0]
            keys[at : at + depth, :] = part[:, :D]
            vals[at : at + depth, :D] = part[:, D:]
            at += depth
    vals[:, D:] = jnp.ones((total, D), BF)
    paged = 4 * CROWS * len(blocks)
    core = lax.axis_index("core")
    lane = lax.broadcasted_iota(jnp.int32, (HALF, D), 1)

    def seen(c):
        return paged + (c + 1) * HALF * len(blocks)

    def scores(h, c):
        s = lax.dot_general(
            q_all[h, c], keys[: seen(c), :], (((1,), (1,)), ((), ())), preferred_element_type=F32
        )
        bias = jnp.where(window_ref[c] > 1, 0.0, bias_ref[...])
        return jnp.concatenate([s[:, :paged] + bias, s[:, paged:]], axis=1)

    def absorb(h, c, s):
        new = jnp.max(s, axis=1, keepdims=True)
        if first:
            new = jnp.broadcast_to(new, (ROWS, D))
        else:
            old = top[h, c]
            new = jnp.maximum(old, new)
        p = jnp.exp2((s - new[:, :1]) * SCALE).astype(BF)
        update = jnp.dot(p, vals[: seen(c), :], preferred_element_type=F32)
        out, norm = update[:, :D], update[:, D:]
        if not first:
            factor = jnp.exp2((old - new) * SCALE)
            out, norm = acc[h, c, :, :D] * factor + out, acc[h, c, :, D:] * factor + norm
        if not last:
            outs[0][h, c, :, :D] = out
            outs[0][h, c, :, D:] = norm
            outs[1][h, c] = new
            return
        out = (out / norm).astype(BF)
        log = new * SCALE + jnp.log2(norm)
        rows = aligned((core + h) & 1, HALF)
        logs = jnp.zeros((HALF, D), F32)
        for g in range(GROUP):
            part = slice(g * HALF, (g + 1) * HALF)
            made[0][c, rows, g * D : (g + 1) * D] = out[part, :]
            left = log[part, :]
            for i in range(3):
                term = left.astype(BF).astype(F32)
                logs = jnp.where(lane == 3 * g + i, term, logs)
                left = left - term
        made[0][c, rows, WIDE:] = logs.astype(BF)

    def token_half(h, carry):
        ahead = scores(h, 3)
        for c in (3, 2, 1, 0):
            now, ahead = ahead, scores(h, c - 1) if c else None
            absorb(h, c, now)
        return carry

    lax.fori_loop(0, 2, token_half, 0)
    if last:
        r = slot()
        for s in range(4):
            outs[s][...] = made[0][r ^ s]


def attend(q, state, pairs, window, bias, last=False):
    total = BLOCK * 8 * len(pairs)
    kept = [] if state is None else list(state)
    work = 16 * ROWS * len(pairs) * (4 * CROWS + 2.5 * HALF)
    if last:
        shapes = [shaped((2 * HALF, WIDE + D))] * 4
    else:
        shapes = [shaped((2, 4, ROWS, 2 * D), F32), shaped((2, 4, ROWS, D), F32)]
    return pl.pallas_call(
        lambda *refs: attend_body(state is None, last, refs),
        in_specs=[smem] + [vmem] * (3 + len(kept) + len(pairs)),
        out_specs=[vmem] * len(shapes),
        out_shape=shapes,
        scratch_shapes=[
            VMEM((2, 4, ROWS, D), BF),
            VMEM((total, D), BF),
            VMEM((total, 2 * D), BF),
        ]
        + ([VMEM((4, 2 * HALF, WIDE + D), BF)] if last else []),
        compiler_params=pltpu.CompilerParams(vmem_limit_bytes=40 * 2**20),
        cost_estimate=pl.CostEstimate(
            flops=int(work * D * 4 * 2), bytes_accessed=2**20, transcendentals=int(work)
        ),
        name="attend",
    )(window, bias, *q, *kept, *pairs)


def merge_body(*refs):
    out = refs[4]
    x = lax.axis_index("x")
    lane = lax.broadcasted_iota(jnp.int32, (D, WIDE), 0)
    head = lax.broadcasted_iota(jnp.int32, (D, WIDE), 1) // D
    pick = jnp.where((lane // 3 == head) & (lane < 3 * GROUP), 1.0, 0.0).astype(BF)
    for pair in range(2):
        one, two = refs[2 * pair], refs[2 * pair + 1]
        a, b = (jnp.dot(ref[:, WIDE:], pick, preferred_element_type=F32) for ref in (one, two))
        most = jnp.maximum(a, b)
        a, b = jnp.exp2(a - most), jnp.exp2(b - most)
        both = (one[:, :WIDE].astype(F32) * a + two[:, :WIDE].astype(F32) * b) / (a + b)
        out[:, aligned((x >> 1) ^ pair, WIDE)] = both.astype(BF)


def merge(messages):
    return pl.pallas_call(
        merge_body, out_shape=shaped((2 * HALF, 2 * WIDE)), name="merge"
    )(*messages)


def spread(s):
    pairs = []
    for x in range(4):
        for core in range(2):
            piece = x ^ s
            pairs.append((x * 2 + core, (2 * core + (piece >> 1)) * 2 + (piece & 1)))
    return pairs


def shift(array, axis, by, size=4):
    return lax.ppermute(array, axis, [(i, (i + by) % size) for i in range(size)])


def swap(array):
    return shift(array, "core", 1, 2)


RING = (0, 2, 3, 1)


def loop_pairs(axis_of_core, by):
    pairs = []
    for zl in range(4):
        for y in range(4):
            for core in range(2):
                z2, y2 = zl, y
                if axis_of_core[core] == "y":
                    y2 = (y + by) % 4
                else:
                    z2 = RING[(RING.index(zl) + by) % 4]
                pairs.append(((zl * 4 + y) * 2 + core, (z2 * 4 + y2) * 2 + core))
    return pairs


def step_on(block, phase, by=1):
    pairs = loop_pairs(("zl", "y") if phase == 0 else ("y", "zl"), by)
    return lax.ppermute(block, ("zl", "y", "core"), pairs)


def cache_bias(page_owner, blocks):
    zl, y, core = lax.axis_index("zl"), lax.axis_index("y"), lax.axis_index("core")
    shape = (4, len(blocks), CROWS)
    xs = lax.broadcasted_iota(jnp.int32, shape, 0)
    n = lax.broadcasted_iota(jnp.int32, shape, 1)
    a = b = jnp.zeros(shape, jnp.int32)
    for i, (a_steps, b_steps) in enumerate(blocks):
        a, b = jnp.where(n == i, a_steps, a), jnp.where(n == i, b_steps, b)
    z_steps, y_steps = jnp.where(core == 0, a, b), jnp.where(core == 0, b, a)
    index = jnp.where(zl == 0, 0, jnp.where(zl == 2, 1, jnp.where(zl == 3, 2, 3)))
    at = (index + 4 - z_steps) & 3
    zs = jnp.where(at == 0, 0, jnp.where(at == 1, 2, jnp.where(at == 2, 3, 1)))
    page = (xs * 4 + zs) * 4 + ((y + 4 - y_steps) & 3)
    page = page.reshape(1, -1, 1)
    late = jnp.any(page == page_owner[None, None, 32:], axis=2)
    return jnp.where(late, 0.0, NEG).astype(F32)


PAIRS = ((0, 1), (3, 2))
PIECES = (
    ((0, 0),),
    ((1, 0), (0, 1)),
    ((1, 1), (0, 2)),
    ((1, 2), (0, 3)),
    ((1, 3),),
)
MOVES = (
    ((0, 1),),
    ((1, 1), (0, 2)),
    ((1, 2), (0, 3)),
    ((1, 3),),
    (),
)


def on_device(queries, keys, values, cache_keys, cache_values, page_owner, window):
    got = [swap(one) for one in (queries, keys, values)]
    start = 4 * D * (1 - lax.axis_index("zh"))
    halves = [lax.dynamic_slice_in_dim(c, start, 4 * D, 1) for c in (cache_keys, cache_values)]
    got.append(shift(jnp.concatenate(halves), "zh", 1, 2))
    messages = deal((queries, keys, values, cache_keys, cache_values), got)
    messages = [messages[0]] + [shift(messages[s], "x", s) for s in range(1, 4)]
    block, mine = join(messages)
    q = [mine, swap(mine)]
    first = step_on(block, 0)
    third = step_on(block, 0, 3)
    second = step_on(first, 0)
    pairs = {(0, 0): jnp.stack([block, first])}
    state = None
    for piece, moves in zip(PIECES, MOVES):
        if state is not None and (1, 0) not in pairs:
            third, second, *state = lax.optimization_barrier((third, second, *state))
            pairs[1, 0] = jnp.stack([third, second])
        for pair, b in moves:
            before = pairs[pair, b - 1]
            if state is not None:
                before, *state = lax.optimization_barrier((before, *state))
            pairs[pair, b] = step_on(before, 1)
        state = attend(
            q,
            state,
            [pairs[one] for one in piece],
            window,
            cache_bias(page_owner, [(a, b) for pair, b in piece for a in PAIRS[pair]]),
            last=piece is PIECES[-1],
        )
    back = [
        lax.ppermute(state[s], ("x", "core"), [(b, a) for a, b in spread(s)]) for s in range(4)
    ]
    return merge(back)


def solution(mesh):
    fine = Mesh(mesh.devices.reshape(4, 4, 4, 2, 2), ("x", "zl", "y", "zh", "core"))
    tokens, heads = ("x", "zl", "y"), ("zh", "core")
    return jax.shard_map(
        on_device,
        mesh=fine,
        in_specs=(
            P(tokens, heads),
            P(tokens, heads),
            P(tokens, heads),
            P(tokens + heads, None),
            P(tokens + heads, None),
            P(),
            P(),
        ),
        out_specs=P(tokens, heads),
        check_vma=False,
    )
```

```python
import jax
import jax.numpy as jnp
from jax import lax
from jax.experimental import pallas as pl
from jax.experimental.pallas import tpu as pltpu
from jax.sharding import Mesh, PartitionSpec as P

D = 128
GROUP = 6
WIDE = GROUP * D
HALF = 64
CROWS = 32
BLOCK = HALF + CROWS
MESSAGE = BLOCK + 3 * HALF
ROWS = GROUP * HALF
NEG = -1e30
SCALE = D**-0.5 * 1.4426950408889634

VMEM = pltpu.VMEM
BF = jnp.bfloat16
F32 = jnp.float32
vmem = pl.BlockSpec(memory_space=VMEM)
smem = pl.BlockSpec(memory_space=pltpu.SMEM)


small = pltpu.CompilerParams(vmem_limit_bytes=8 * 2**20)


def shaped(shape, dtype=BF):
    return jax.ShapeDtypeStruct(shape, dtype)


def slot():
    return 2 * (lax.axis_index("x") & 1) + lax.axis_index("core")


def aligned(index, step):
    return pl.ds(pl.multiple_of(index * step, step), step)


def from_one_core(head, q, k, v, out):
    rows, e = aligned(lax.axis_index("core"), HALF), head & 1
    out[:HALF, :D] = k[rows, aligned(e, D)]
    out[:HALF, D:] = v[rows, aligned(e, D)]
    for i in range(3):
        lanes = pl.ds(pl.multiple_of(e * WIDE + i * 2 * D, D), 2 * D)
        out[BLOCK + i * HALF : BLOCK + (i + 1) * HALF, :] = q[rows, lanes]


def deal_body(q_ref, k_ref, v_ref, ck_ref, cv_ref, *outs):
    x, half, core = lax.axis_index("x"), lax.axis_index("zh"), lax.axis_index("core")
    for s in range(4):
        head, out = (x + s) & 3, outs[s]

        @pl.when((head >> 1) == core)
        def _(head=head, out=out):
            from_one_core(head, q_ref, k_ref, v_ref, out)

        lanes = aligned(half * 4 + head, D)
        out[HALF : HALF + 16, :D] = ck_ref[:, lanes]
        out[HALF : HALF + 16, D:] = cv_ref[:, lanes]


def deal(*own):
    return pl.pallas_call(
        deal_body,
        in_specs=[vmem] * len(own),
        out_specs=[vmem] * 4,
        out_shape=[shaped((MESSAGE, 2 * D))] * 4,
        compiler_params=small,
        name="deal",
    )(*own)


def fill_body(q_got, k_got, v_got, c_got, *refs):
    x, core = lax.axis_index("x"), lax.axis_index("core")
    for s in range(4):
        head, mine, out = (x + s) & 3, refs[s], refs[4 + s]

        @pl.when((head >> 1) == core)
        def _(mine=mine, out=out):
            out[:HALF, :] = mine[:HALF, :]
            out[BLOCK:, :] = mine[BLOCK:, :]

        @pl.when((head >> 1) != core)
        def _(head=head, out=out):
            from_one_core(head, q_got, k_got, v_got, out)

        lanes = aligned(head, D)
        out[HALF : HALF + 16, :] = mine[HALF : HALF + 16, :]
        out[HALF + 16 : BLOCK, :D] = c_got[:16, lanes]
        out[HALF + 16 : BLOCK, D:] = c_got[16:, lanes]


def fill(got, messages):
    return pl.pallas_call(
        fill_body,
        in_specs=[vmem] * 8,
        out_specs=[vmem] * 4,
        out_shape=[shaped((MESSAGE, 2 * D))] * 4,
        compiler_params=small,
        name="fill",
    )(*got, *messages)


def join_body(*refs):
    x = lax.axis_index("x")
    block, q = refs[4:]
    for s in range(4):
        source = pl.ds((x + 4 - s) & 3, 1)
        block[source] = refs[s][:BLOCK, :][None]
        q[source] = refs[s][BLOCK:, :][None]


def join(messages):
    return pl.pallas_call(
        join_body,
        in_specs=[vmem] * 4,
        out_specs=[vmem] * 2,
        out_shape=[shaped((4, BLOCK, 2 * D)), shaped((4, 3 * HALF, 2 * D))],
        compiler_params=small,
        name="join",
    )(*messages)


def attend_body(first, last, refs):
    window_ref, bias_ref, *refs = refs
    q_refs, refs = refs[:2], refs[2:]
    if not first:
        acc, top, *refs = refs
    q_all, keys, vals, *made = refs[-4:] if last else refs[-3:]
    blocks, outs = (refs[:-8], refs[-8:-4]) if last else (refs[:-5], refs[-5:-3])
    blocks = [pair.at[i] for pair in blocks for i in range(2)]
    total = keys.shape[0]
    for h in range(2):
        for c in range(4):
            for g in range(GROUP):
                rows = slice(g // 2 * HALF, (g // 2 + 1) * HALF)
                part = q_refs[h][c, rows, g % 2 * D : (g % 2 + 1) * D]
                q_all[h, c, g * HALF : (g + 1) * HALF, :] = part
    at = 0
    for t in range(-4, 4):
        for block in blocks:
            part = block[t + 4, HALF:, :] if t < 0 else block[t, :HALF, :]
            depth = part.shape[0]
            keys[at : at + depth, :] = part[:, :D]
            vals[at : at + depth, :D] = part[:, D:]
            at += depth
    vals[:, D:] = jnp.ones((total, D), BF)
    paged = 4 * CROWS * len(blocks)
    core = lax.axis_index("core")
    lane = lax.broadcasted_iota(jnp.int32, (HALF, D), 1)

    def seen(c):
        return paged + (c + 1) * HALF * len(blocks)

    def scores(h, c):
        s = lax.dot_general(
            q_all[h, c], keys[: seen(c), :], (((1,), (1,)), ((), ())), preferred_element_type=F32
        )
        bias = jnp.where(window_ref[c] > 1, 0.0, bias_ref[...])
        return jnp.concatenate([s[:, :paged] + bias, s[:, paged:]], axis=1)

    def absorb(h, c, s):
        new = jnp.max(s, axis=1, keepdims=True)
        if first:
            new = jnp.broadcast_to(new, (ROWS, D))
        else:
            old = top[h, c]
            new = jnp.maximum(old, new)
        p = jnp.exp2((s - new[:, :1]) * SCALE).astype(BF)
        update = jnp.dot(p, vals[: seen(c), :], preferred_element_type=F32)
        out, norm = update[:, :D], update[:, D:]
        if not first:
            factor = jnp.exp2((old - new) * SCALE)
            out, norm = acc[h, c, :, :D] * factor + out, acc[h, c, :, D:] * factor + norm
        if not last:
            outs[0][h, c, :, :D] = out
            outs[0][h, c, :, D:] = norm
            outs[1][h, c] = new
            return
        out = (out / norm).astype(BF)
        log = new * SCALE + jnp.log2(norm)
        rows = aligned((core + h) & 1, HALF)
        logs = jnp.zeros((HALF, D), F32)
        for g in range(GROUP):
            part = slice(g * HALF, (g + 1) * HALF)
            made[0][c, rows, g * D : (g + 1) * D] = out[part, :]
            left = log[part, :]
            for i in range(3):
                term = left.astype(BF).astype(F32)
                logs = jnp.where(lane == 3 * g + i, term, logs)
                left = left - term
        made[0][c, rows, WIDE:] = logs.astype(BF)

    def token_half(h, carry):
        ahead = scores(h, 3)
        for c in (3, 2, 1, 0):
            now, ahead = ahead, scores(h, c - 1) if c else None
            absorb(h, c, now)
        return carry

    lax.fori_loop(0, 2, token_half, 0)
    if last:
        r = slot()
        for s in range(4):
            outs[s][...] = made[0][r ^ s]


def attend(q, state, pairs, window, bias, last=False):
    total = BLOCK * 8 * len(pairs)
    kept = [] if state is None else list(state)
    work = 16 * ROWS * len(pairs) * (4 * CROWS + 2.5 * HALF)
    if last:
        shapes = [shaped((2 * HALF, WIDE + D))] * 4
    else:
        shapes = [shaped((2, 4, ROWS, 2 * D), F32), shaped((2, 4, ROWS, D), F32)]
    return pl.pallas_call(
        lambda *refs: attend_body(state is None, last, refs),
        in_specs=[smem] + [vmem] * (3 + len(kept) + len(pairs)),
        out_specs=[vmem] * len(shapes),
        out_shape=shapes,
        scratch_shapes=[
            VMEM((2, 4, ROWS, D), BF),
            VMEM((total, D), BF),
            VMEM((total, 2 * D), BF),
        ]
        + ([VMEM((4, 2 * HALF, WIDE + D), BF)] if last else []),
        compiler_params=pltpu.CompilerParams(vmem_limit_bytes=40 * 2**20),
        cost_estimate=pl.CostEstimate(
            flops=int(work * D * 4 * 2), bytes_accessed=2**20, transcendentals=int(work)
        ),
        name="attend",
    )(window, bias, *q, *kept, *pairs)


def merge_body(*refs):
    out = refs[4]
    x = lax.axis_index("x")
    lane = lax.broadcasted_iota(jnp.int32, (D, WIDE), 0)
    head = lax.broadcasted_iota(jnp.int32, (D, WIDE), 1) // D
    pick = jnp.where((lane // 3 == head) & (lane < 3 * GROUP), 1.0, 0.0).astype(BF)
    for pair in range(2):
        one, two = refs[2 * pair], refs[2 * pair + 1]
        a, b = (jnp.dot(ref[:, WIDE:], pick, preferred_element_type=F32) for ref in (one, two))
        most = jnp.maximum(a, b)
        a, b = jnp.exp2(a - most), jnp.exp2(b - most)
        both = (one[:, :WIDE].astype(F32) * a + two[:, :WIDE].astype(F32) * b) / (a + b)
        out[:, aligned((x >> 1) ^ pair, WIDE)] = both.astype(BF)


def merge(messages):
    return pl.pallas_call(
        merge_body,
        in_specs=[vmem] * 4,
        out_specs=vmem,
        out_shape=shaped((2 * HALF, 2 * WIDE)),
        compiler_params=small,
        name="merge",
    )(*messages)


def spread(s):
    pairs = []
    for x in range(4):
        for core in range(2):
            piece = x ^ s
            pairs.append((x * 2 + core, (2 * core + (piece >> 1)) * 2 + (piece & 1)))
    return pairs


def shift(array, axis, by, size=4):
    return lax.ppermute(array, axis, [(i, (i + by) % size) for i in range(size)])


def swap(array):
    return shift(array, "core", 1, 2)


RING = (0, 2, 3, 1)


def loop_pairs(axis_of_core, by):
    pairs = []
    for zl in range(4):
        for y in range(4):
            for core in range(2):
                z2, y2 = zl, y
                if axis_of_core[core] == "y":
                    y2 = (y + by) % 4
                else:
                    z2 = RING[(RING.index(zl) + by) % 4]
                pairs.append(((zl * 4 + y) * 2 + core, (z2 * 4 + y2) * 2 + core))
    return pairs


def step_on(block, phase, by=1):
    pairs = loop_pairs(("zl", "y") if phase == 0 else ("y", "zl"), by)
    return lax.ppermute(block, ("zl", "y", "core"), pairs)


def cache_bias(page_owner, blocks):
    zl, y, core = lax.axis_index("zl"), lax.axis_index("y"), lax.axis_index("core")
    shape = (4, len(blocks), CROWS)
    xs = lax.broadcasted_iota(jnp.int32, shape, 0)
    n = lax.broadcasted_iota(jnp.int32, shape, 1)
    a = b = jnp.zeros(shape, jnp.int32)
    for i, (a_steps, b_steps) in enumerate(blocks):
        a, b = jnp.where(n == i, a_steps, a), jnp.where(n == i, b_steps, b)
    z_steps, y_steps = jnp.where(core == 0, a, b), jnp.where(core == 0, b, a)
    index = jnp.where(zl == 0, 0, jnp.where(zl == 2, 1, jnp.where(zl == 3, 2, 3)))
    at = (index + 4 - z_steps) & 3
    zs = jnp.where(at == 0, 0, jnp.where(at == 1, 2, jnp.where(at == 2, 3, 1)))
    page = (xs * 4 + zs) * 4 + ((y + 4 - y_steps) & 3)
    page = page.reshape(1, -1, 1)
    late = jnp.any(page == page_owner[None, None, 32:], axis=2)
    return jnp.where(late, 0.0, NEG).astype(F32)


PAIRS = ((0, 1), (3, 2))
PIECES = (
    ((0, 0),),
    ((1, 0), (0, 1)),
    ((1, 1), (0, 2)),
    ((1, 2), (0, 3)),
    ((1, 3),),
)
MOVES = (
    ((0, 1),),
    ((1, 1), (0, 2)),
    ((1, 2), (0, 3)),
    ((1, 3),),
    (),
)


def on_device(queries, keys, values, cache_keys, cache_values, page_owner, window):
    got = [swap(one) for one in (queries, keys, values)]
    start = 4 * D * (1 - lax.axis_index("zh"))
    halves = [lax.dynamic_slice_in_dim(c, start, 4 * D, 1) for c in (cache_keys, cache_values)]
    got.append(shift(jnp.concatenate(halves), "zh", 1, 2))
    messages = fill(got, deal(queries, keys, values, cache_keys, cache_values))
    messages = [messages[0]] + [shift(messages[s], "x", s) for s in range(1, 4)]
    block, mine = join(messages)
    q = [mine, swap(mine)]
    first = step_on(block, 0)
    third = step_on(block, 0, 3)
    second = step_on(first, 0)
    pairs = {(0, 0): jnp.stack([block, first])}
    state = None
    for piece, moves in zip(PIECES, MOVES):
        if state is not None and (1, 0) not in pairs:
            third, second, *state = lax.optimization_barrier((third, second, *state))
            pairs[1, 0] = jnp.stack([third, second])
        for pair, b in moves:
            before = pairs[pair, b - 1]
            if state is not None:
                before, *state = lax.optimization_barrier((before, *state))
            pairs[pair, b] = step_on(before, 1)
        state = attend(
            q,
            state,
            [pairs[one] for one in piece],
            window,
            cache_bias(page_owner, [(a, b) for pair, b in piece for a in PAIRS[pair]]),
            last=piece is PIECES[-1],
        )
    back = [
        lax.ppermute(state[s], ("x", "core"), [(b, a) for a, b in spread(s)]) for s in range(4)
    ]
    return merge(back)


def solution(mesh):
    fine = Mesh(mesh.devices.reshape(4, 4, 4, 2, 2), ("x", "zl", "y", "zh", "core"))
    tokens, heads = ("x", "zl", "y"), ("zh", "core")
    return jax.shard_map(
        on_device,
        mesh=fine,
        in_specs=(
            P(tokens, heads),
            P(tokens, heads),
            P(tokens, heads),
            P(tokens + heads, None),
            P(tokens + heads, None),
            P(),
            P(),
        ),
        out_specs=P(tokens, heads),
        check_vma=False,
    )
```

```python
import jax
import jax.numpy as jnp
from jax import lax
from jax.experimental import pallas as pl
from jax.experimental.pallas import tpu as pltpu
from jax.sharding import Mesh, PartitionSpec as P

D = 128
GROUP = 6
WIDE = GROUP * D
HALF = 64
CROWS = 32
BLOCK = HALF + CROWS
MESSAGE = BLOCK + 3 * HALF
ROWS = GROUP * HALF
NEG = -1e30
SCALE = D**-0.5 * 1.4426950408889634

VMEM = pltpu.VMEM
BF = jnp.bfloat16
F32 = jnp.float32
vmem = pl.BlockSpec(memory_space=VMEM)
smem = pl.BlockSpec(memory_space=pltpu.SMEM)


small = pltpu.CompilerParams(vmem_limit_bytes=8 * 2**20)


def shaped(shape, dtype=BF):
    return jax.ShapeDtypeStruct(shape, dtype)


def slot():
    return 2 * (lax.axis_index("x") & 1) + lax.axis_index("core")


def aligned(index, step):
    return pl.ds(pl.multiple_of(index * step, step), step)


def from_one_core(head, q, k, v, out):
    rows, e = aligned(lax.axis_index("core"), HALF), head & 1
    out[:HALF, :D] = k[rows, aligned(e, D)]
    out[:HALF, D:] = v[rows, aligned(e, D)]
    for i in range(3):
        lanes = pl.ds(pl.multiple_of(e * WIDE + i * 2 * D, D), 2 * D)
        out[BLOCK + i * HALF : BLOCK + (i + 1) * HALF, :] = q[rows, lanes]


def deal_body(q_ref, kv_ref, c_ref, *outs):
    x, core = lax.axis_index("x"), lax.axis_index("core")
    k_ref, v_ref = kv_ref.at[:, : 2 * D], kv_ref.at[:, 2 * D :]
    for s in range(4):
        head, out = (x + s) & 3, outs[s]

        @pl.when((head >> 1) == core)
        def _(head=head, out=out):
            from_one_core(head, q_ref, k_ref, v_ref, out)

        lanes = aligned(head, D)
        out[HALF : HALF + 16, :D] = c_ref[:16, lanes]
        out[HALF : HALF + 16, D:] = c_ref[16:, lanes]


def deal(*own):
    return pl.pallas_call(
        deal_body,
        in_specs=[vmem] * len(own),
        out_specs=[vmem] * 4,
        out_shape=[shaped((MESSAGE, 2 * D))] * 4,
        compiler_params=small,
        name="deal",
    )(*own)


def fill_body(q_got, k_got, v_got, c_got, *refs):
    x, core = lax.axis_index("x"), lax.axis_index("core")
    for s in range(4):
        head, mine, out = (x + s) & 3, refs[s], refs[4 + s]

        @pl.when((head >> 1) == core)
        def _(mine=mine, out=out):
            out[:HALF, :] = mine[:HALF, :]
            out[BLOCK:, :] = mine[BLOCK:, :]

        @pl.when((head >> 1) != core)
        def _(head=head, out=out):
            from_one_core(head, q_got, k_got, v_got, out)

        lanes = aligned(head, D)
        out[HALF : HALF + 16, :] = mine[HALF : HALF + 16, :]
        out[HALF + 16 : BLOCK, :D] = c_got[:16, lanes]
        out[HALF + 16 : BLOCK, D:] = c_got[16:, lanes]


def fill(got, messages):
    return pl.pallas_call(
        fill_body,
        in_specs=[vmem] * 8,
        out_specs=[vmem] * 4,
        out_shape=[shaped((MESSAGE, 2 * D))] * 4,
        compiler_params=small,
        name="fill",
    )(*got, *messages)


def join_body(*refs):
    x = lax.axis_index("x")
    block, q = refs[4:]
    for s in range(4):
        source = pl.ds((x + 4 - s) & 3, 1)
        block[source] = refs[s][:BLOCK, :][None]
        q[source] = refs[s][BLOCK:, :][None]


def join(messages):
    return pl.pallas_call(
        join_body,
        in_specs=[vmem] * 4,
        out_specs=[vmem] * 2,
        out_shape=[shaped((4, BLOCK, 2 * D)), shaped((4, 3 * HALF, 2 * D))],
        compiler_params=small,
        name="join",
    )(*messages)


def attend_body(first, last, refs):
    window_ref, bias_ref, *refs = refs
    q_refs, refs = refs[:2], refs[2:]
    if not first:
        acc, top, *refs = refs
    ending = last is not None
    q_all, keys, vals = refs[-3:]
    blocks, outs = (refs[:-4], refs[-4:-3]) if ending else (refs[:-5], refs[-5:-3])
    blocks = [pair.at[i] for pair in blocks for i in range(2)]
    total = keys.shape[0]
    for h in [last] if ending else range(2):
        for c in range(4):
            for g in range(GROUP):
                rows = slice(g // 2 * HALF, (g // 2 + 1) * HALF)
                part = q_refs[h][c, rows, g % 2 * D : (g % 2 + 1) * D]
                q_all[h, c, g * HALF : (g + 1) * HALF, :] = part
    at = 0
    for t in range(-4, 4):
        for block in blocks:
            part = block[t + 4, HALF:, :] if t < 0 else block[t, :HALF, :]
            depth = part.shape[0]
            keys[at : at + depth, :] = part[:, :D]
            vals[at : at + depth, :D] = part[:, D:]
            at += depth
    vals[:, D:] = jnp.ones((total, D), BF)
    paged = 4 * CROWS * len(blocks)
    lane = lax.broadcasted_iota(jnp.int32, (HALF, D), 1)

    def seen(c):
        return paged + (c + 1) * HALF * len(blocks)

    def scores(h, c):
        s = lax.dot_general(
            q_all[h, c], keys[: seen(c), :], (((1,), (1,)), ((), ())), preferred_element_type=F32
        )
        bias = jnp.where(window_ref[c] > 1, 0.0, bias_ref[...])
        return jnp.concatenate([s[:, :paged] + bias, s[:, paged:]], axis=1)

    def absorb(h, c, s):
        new = jnp.max(s, axis=1, keepdims=True)
        if first:
            new = jnp.broadcast_to(new, (ROWS, D))
        else:
            old = top[h, c]
            new = jnp.maximum(old, new)
        p = jnp.exp2((s - new[:, :1]) * SCALE).astype(BF)
        update = jnp.dot(p, vals[: seen(c), :], preferred_element_type=F32)
        out, norm = update[:, :D], update[:, D:]
        if not first:
            factor = jnp.exp2((old - new) * SCALE)
            out, norm = acc[h, c, :, :D] * factor + out, acc[h, c, :, D:] * factor + norm
        if not ending:
            outs[0][h, c, :, :D] = out
            outs[0][h, c, :, D:] = norm
            outs[1][h, c] = new
            return
        out = (out / norm).astype(BF)
        log = new * SCALE + jnp.log2(norm)
        logs = jnp.zeros((HALF, D), F32)
        for g in range(GROUP):
            part = slice(g * HALF, (g + 1) * HALF)
            outs[0][c, :, g * D : (g + 1) * D] = out[part, :]
            left = log[part, :]
            for i in range(3):
                term = left.astype(BF).astype(F32)
                logs = jnp.where(lane == 3 * g + i, term, logs)
                left = left - term
        outs[0][c, :, WIDE:] = logs.astype(BF)

    def token_half(h, carry):
        ahead = scores(h, 3)
        for c in (3, 2, 1, 0):
            now, ahead = ahead, scores(h, c - 1) if c else None
            absorb(h, c, now)
        return carry

    if ending:
        token_half(last, 0)
    else:
        lax.fori_loop(0, 2, token_half, 0)


def attend(q, state, pairs, window, bias, last=None):
    total = BLOCK * 8 * len(pairs)
    kept = [] if state is None else list(state)
    work = 16 * ROWS * len(pairs) * (4 * CROWS + 2.5 * HALF)
    if last is not None:
        shapes = [shaped((4, HALF, WIDE + D))]
    else:
        shapes = [shaped((2, 4, ROWS, 2 * D), F32), shaped((2, 4, ROWS, D), F32)]
    return pl.pallas_call(
        lambda *refs: attend_body(state is None, last, refs),
        in_specs=[smem] + [vmem] * (3 + len(kept) + len(pairs)),
        out_specs=[vmem] * len(shapes),
        out_shape=shapes,
        scratch_shapes=[
            VMEM((2, 4, ROWS, D), BF),
            VMEM((total, D), BF),
            VMEM((total, 2 * D), BF),
        ],
        compiler_params=pltpu.CompilerParams(vmem_limit_bytes=40 * 2**20),
        cost_estimate=pl.CostEstimate(
            flops=int(work * D * 4 * 2), bytes_accessed=2**20, transcendentals=int(work)
        ),
        name="attend",
    )(window, bias, *q, *kept, *pairs)


def merge_body(one, two, *outs):
    r = slot()
    lane = lax.broadcasted_iota(jnp.int32, (D, WIDE), 0)
    head = lax.broadcasted_iota(jnp.int32, (D, WIDE), 1) // D
    pick = jnp.where((lane // 3 == head) & (lane < 3 * GROUP), 1.0, 0.0).astype(BF)
    for s in range(4):
        refs = one[r ^ s], two[r ^ s]
        a, b = (jnp.dot(ref[:, WIDE:], pick, preferred_element_type=F32) for ref in refs)
        most = jnp.maximum(a, b)
        a, b = jnp.exp2(a - most), jnp.exp2(b - most)
        both = (refs[0][:, :WIDE].astype(F32) * a + refs[1][:, :WIDE].astype(F32) * b) / (a + b)
        outs[s][...] = both.astype(BF)


def merge(one, two):
    return pl.pallas_call(
        merge_body,
        in_specs=[vmem] * 2,
        out_specs=[vmem] * 4,
        out_shape=[shaped((HALF, WIDE))] * 4,
        compiler_params=small,
        name="merge",
    )(one, two)


def place_body(*refs):
    x = lax.axis_index("x")
    for s in range(4):
        piece = x ^ s
        refs[4][aligned(piece & 1, HALF), aligned(piece >> 1, WIDE)] = refs[s][...]


def place(pieces):
    return pl.pallas_call(
        place_body,
        in_specs=[vmem] * 4,
        out_specs=vmem,
        out_shape=shaped((2 * HALF, 2 * WIDE)),
        compiler_params=small,
        name="place",
    )(*pieces)


def spread(s):
    pairs = []
    for x in range(4):
        for core in range(2):
            piece = x ^ s
            pairs.append((x * 2 + core, (2 * core + (piece >> 1)) * 2 + (piece & 1)))
    return pairs


def shift(array, axis, by, size=4):
    return lax.ppermute(array, axis, [(i, (i + by) % size) for i in range(size)])


def swap(array):
    return shift(array, "core", 1, 2)


RING = (0, 2, 3, 1)


def loop_pairs(axis_of_core, by):
    pairs = []
    for zl in range(4):
        for y in range(4):
            for core in range(2):
                z2, y2 = zl, y
                if axis_of_core[core] == "y":
                    y2 = (y + by) % 4
                else:
                    z2 = RING[(RING.index(zl) + by) % 4]
                pairs.append(((zl * 4 + y) * 2 + core, (z2 * 4 + y2) * 2 + core))
    return pairs


def step_on(block, phase, by=1):
    pairs = loop_pairs(("zl", "y") if phase == 0 else ("y", "zl"), by)
    return lax.ppermute(block, ("zl", "y", "core"), pairs)


def cache_bias(page_owner, blocks):
    zl, y, core = lax.axis_index("zl"), lax.axis_index("y"), lax.axis_index("core")
    shape = (4, len(blocks), CROWS)
    xs = lax.broadcasted_iota(jnp.int32, shape, 0)
    n = lax.broadcasted_iota(jnp.int32, shape, 1)
    a = b = jnp.zeros(shape, jnp.int32)
    for i, (a_steps, b_steps) in enumerate(blocks):
        a, b = jnp.where(n == i, a_steps, a), jnp.where(n == i, b_steps, b)
    z_steps, y_steps = jnp.where(core == 0, a, b), jnp.where(core == 0, b, a)
    index = jnp.where(zl == 0, 0, jnp.where(zl == 2, 1, jnp.where(zl == 3, 2, 3)))
    at = (index + 4 - z_steps) & 3
    zs = jnp.where(at == 0, 0, jnp.where(at == 1, 2, jnp.where(at == 2, 3, 1)))
    page = (xs * 4 + zs) * 4 + ((y + 4 - y_steps) & 3)
    page = page.reshape(1, -1, 1)
    late = jnp.any(page == page_owner[None, None, 32:], axis=2)
    return jnp.where(late, 0.0, NEG).astype(F32)


PAIRS = ((0, 1), (3, 2))
PIECES = (
    ((0, 0),),
    ((1, 0), (0, 1)),
    ((1, 1), (0, 2)),
    ((1, 2), (0, 3)),
    ((1, 3),),
)
MOVES = (
    ((0, 1),),
    ((1, 1), (0, 2)),
    ((1, 2), (0, 3)),
    ((1, 3),),
    (),
)


def on_device(queries, keys, values, cache_keys, cache_values, page_owner, window):
    got = [swap(one) for one in (queries, keys, values)]
    half = lax.axis_index("zh")
    own, other = (
        jnp.concatenate(
            [lax.dynamic_slice_in_dim(c, 4 * D * h, 4 * D, 1) for c in (cache_keys, cache_values)]
        )
        for h in (half, 1 - half)
    )
    got.append(shift(other, "zh", 1, 2))
    messages = fill(got, deal(queries, jnp.concatenate([keys, values], axis=1), own))
    messages = [messages[0]] + [shift(messages[s], "x", s) for s in range(1, 4)]
    block, mine = join(messages)
    q = [mine, swap(mine)]
    first = step_on(block, 0)
    third = step_on(block, 0, 3)
    second = step_on(first, 0)
    pairs = {(0, 0): jnp.stack([block, first])}
    state = None
    for piece, moves in zip(PIECES, MOVES):
        if state is not None and (1, 0) not in pairs:
            third, second, *state = lax.optimization_barrier((third, second, *state))
            pairs[1, 0] = jnp.stack([third, second])
        for pair, b in moves:
            before = pairs[pair, b - 1]
            if state is not None:
                before, *state = lax.optimization_barrier((before, *state))
            pairs[pair, b] = step_on(before, 1)
        parts = [pairs[one] for one in piece]
        bias = cache_bias(page_owner, [(a, b) for pair, b in piece for a in PAIRS[pair]])
        if piece is not PIECES[-1]:
            state = attend(q, state, parts, window, bias)
    (theirs,) = attend(q, state, parts, window, bias, last=1)
    theirs, *state = lax.optimization_barrier((theirs, *state))
    theirs = swap(theirs)
    (mine,) = attend(q, state, parts, window, bias, last=0)
    pieces = merge(mine, theirs)
    back = [
        lax.ppermute(pieces[s], ("x", "core"), [(b, a) for a, b in spread(s)]) for s in range(4)
    ]
    return place(back)


def solution(mesh):
    fine = Mesh(mesh.devices.reshape(4, 4, 4, 2, 2), ("x", "zl", "y", "zh", "core"))
    tokens, heads = ("x", "zl", "y"), ("zh", "core")
    return jax.shard_map(
        on_device,
        mesh=fine,
        in_specs=(
            P(tokens, heads),
            P(tokens, heads),
            P(tokens, heads),
            P(tokens + heads, None),
            P(tokens + heads, None),
            P(),
            P(),
        ),
        out_specs=P(tokens, heads),
        check_vma=False,
    )
```
